32 devices in a mesh: row: 4 (over y, core), col: 8 (over z, x).
Axes of the slice: x: 2, y: 2, z: 4, core: 2. Of those that a mesh axis runs over, the one named last changes fastest.
Arguments:
- prompt_token_states: bfloat16 [896, 5120], P('col', 'row'), may hold values from -960 to 960
- gain: bfloat16 [5120], P('row'), may hold values from 0.25 to 1.75
- projection_weight: bfloat16 [5120, 2, 5120], P('col', None, 'row'), may hold values from -0.078125 to 0.078125
- adapter_down_maps: bfloat16 [8, 5120, 256], P('col', 'row'), may hold values from -0.078125 to 0.078125
- adapter_up_maps: bfloat16 [8, 2, 128, 5120], P('col', None, None, 'row'), may hold values from -0.5 to 0.5
- prompt_token_length: int32 [12], replicated, may hold values from 1 to 134, 896 in all
- prompt_of_request: int32 [144], replicated, may hold values from 0 to 11, never falling along the last dimension, each value on 1 to 16 neighbouring positions
- adapter_of_request: int32 [144], replicated, may hold values from 0 to 31, as said below
- adapter_slot_index: int32 [32], replicated, may hold values from -1 to 7, as said below
Outputs:
- query_rows: bfloat16 [896, 16, 5120], P('col', None, 'row')
- value_rows: bfloat16 [896, 16, 5120], P('col', None, 'row')
The draws below stay inside these ranges and needn't reach their ends.
Inputs may be any that keep to these rules, and one draw needn't show every extreme that they name: `adapter_of_request`: every request names a loaded adapter (adapter_slot_index not -1), and every slot 0 to 7 is named by some request. `adapter_slot_index`: the values other than -1 are 0 to 7, each once; the others are -1. `prompt_of_request`: requests of one prompt stand together, prompts in rising order; each prompt has 1 to 16 requests.
All inputs are finite; a program needn't handle non-finite values.
Results may differ from the reference program's by a relative error of at most 0.0057.
Values may be sent and summed in bfloat16 or wider, within the bound.
No kernel may reach another device: no remote copies, remote signals or barrier semaphores. Data moves between devices by JAX's collectives and lax.ppermute only.
A program may use at most 128 MiB of HBM per device.

```python
import math
import jax
import jax.numpy as jnp
import numpy as np
from jax import lax

MODEL_WIDTH = 5120
ADAPTER_RANK = 128
SLOTS = 16
PROMPTS = 12
REQS = 144
PTOK = 896
LMAX = 134
LIVE_ADAPTERS = 8
ADAPTERS = 32
N_COL = 8


def adapter_order(key):
    middle = 1 + jax.random.permutation(jax.random.fold_in(key, 11), ADAPTERS - 2)
    ends = jnp.array([ADAPTERS - 1, 0], dtype=jnp.int32)
    order = jnp.concatenate([ends, middle.astype(jnp.int32)])
    live_part = order[:LIVE_ADAPTERS][jax.random.permutation(jax.random.fold_in(key, 15), LIVE_ADAPTERS)]
    return jnp.concatenate([live_part, order[LIVE_ADAPTERS:]]).astype(jnp.int32)


def draw_adapter_slot_index(key, part):
    order = adapter_order(key)
    place = jnp.argsort(order).astype(jnp.int32)
    return jnp.where(place < LIVE_ADAPTERS, place, -1).astype(jnp.int32)


def draw_adapter_of_request(key, part):
    order = adapter_order(key)
    cover = jax.random.permutation(jax.random.fold_in(key, 12), LIVE_ADAPTERS)
    others = jax.random.randint(jax.random.fold_in(key, 13), (REQS,), 0, LIVE_ADAPTERS)
    index = jnp.arange(REQS)
    chosen = jnp.where(index < LIVE_ADAPTERS, cover[jnp.minimum(index, LIVE_ADAPTERS - 1)], others)
    shuffle = jax.random.permutation(jax.random.fold_in(key, 14), REQS)
    return order[chosen[shuffle]].astype(jnp.int32)


def draw_prompt_token_states(key, part):
    first = jax.random.fold_in(key, 1)
    second = jax.random.fold_in(key, 2)
    columns = 10.0 ** (jnp.arange(MODEL_WIDTH, dtype=jnp.float32) / MODEL_WIDTH)
    mixed = jnp.clip(jax.random.normal(first, (PTOK, MODEL_WIDTH), jnp.float32), -4.0, 4.0)
    rows = jnp.exp(jax.random.uniform(second, (PTOK, 1), jnp.float32, 0.0, math.log(10.0)))
    columns = columns[None, :]
    return (mixed * rows * columns).astype(jnp.bfloat16)


def shard_levels(own_key, shape, cuts, least, largest):
    level, own = 1.0, jax.random.fold_in(own_key, 6)
    for axis_at, parts in cuts:
        heights = jnp.exp(jax.random.uniform(jax.random.fold_in(own, axis_at), (parts,), jnp.float32, least / len(cuts), largest / len(cuts)))
        level = level * jnp.repeat(heights, shape[axis_at] // parts).reshape([-1 if axis == axis_at else 1 for axis in range(len(shape))])
    return level


def split_up(number_of, total, most, lean):
    loads = [(1 << 20) // math.isqrt(standing ** lean) + 1 for standing in range(2, number_of + 1)]
    rest, given = total - most - (number_of - 1), [1] * (number_of - 1)
    while rest > 0:
        free = [i for i in range(number_of - 1) if given[i] < most]
        whole, budget = sum([loads[i] for i in free]), rest
        for i in free:
            addition = min(most - given[i], max(1, budget * loads[i] // whole), rest)
            given[i] = given[i] + addition
            rest = rest - addition
    return np.array([most] + given)


def uneven(rng, count, total, reach, lean):
    if count == 2:
        one = jax.random.randint(rng, (), max(1, total - reach), min(reach, total - 1) + 1)
        return jnp.stack([one, total - one])
    tallies = jnp.asarray(split_up(count, total, reach, lean), jnp.int32)
    couples = (count - 1) // 2
    giver, sink = tallies[1:1 + 2 * couples:2], tallies[2:2 + 2 * couples:2]
    slack = jnp.minimum(giver - 1, reach - sink)
    moved = jax.random.randint(jax.random.fold_in(rng, 1), (couples,), 0, 1 << 20) % (slack + 1)
    tallies = tallies.at[1:1 + 2 * couples:2].set(giver - moved).at[2:2 + 2 * couples:2].set(sink + moved)
    return tallies[jax.random.permutation(jax.random.fold_in(rng, 2), count)]


def centred(rng, dims, width, most, split=(), kind=jnp.bfloat16):
    level = shard_levels(rng, dims, split, -0.22, 0.18) if split else 1.0
    values = jax.random.normal(rng, dims, jnp.float32) * width * level
    return jnp.minimum(jnp.maximum(values, -most), most).astype(kind)


def setup_inputs(seed: int = 0) -> dict:
    splits = jax.random.split(jax.random.key(seed), 10)
    prompt_token_states = draw_prompt_token_states(jax.random.fold_in(splits[9], 71), 0)
    gain = jnp.clip(1.0 + 0.15 * jax.random.normal(splits[1], (MODEL_WIDTH,), jnp.float32), 0.25, 1.75).astype(jnp.bfloat16)
    projection_weight = centred(splits[2], (MODEL_WIDTH, 2, MODEL_WIDTH), MODEL_WIDTH ** -0.5, 0.078125, ((0, 8), (2, 4)))
    adapter_down_maps = centred(splits[3], (LIVE_ADAPTERS, MODEL_WIDTH, 2 * ADAPTER_RANK), MODEL_WIDTH ** -0.5, 0.078125, ((0, 8), (1, 4)))
    adapter_up_maps = centred(splits[4], (LIVE_ADAPTERS, 2, ADAPTER_RANK, MODEL_WIDTH), ADAPTER_RANK ** -0.5, 0.5, ((0, 8), (3, 4)))
    prompt_token_length = uneven(splits[5], PROMPTS, PTOK, LMAX, 1).astype(jnp.int32)
    prompt_of_request = jnp.searchsorted(jnp.cumsum(uneven(splits[6], PROMPTS, REQS, SLOTS, 1)), jnp.arange(REQS), side="right").astype(jnp.int32)
    adapter_of_request = draw_adapter_of_request(jax.random.fold_in(splits[9], 71), 0)
    adapter_slot_index = draw_adapter_slot_index(jax.random.fold_in(splits[9], 71), 0)
    return dict(prompt_token_states=prompt_token_states, gain=gain, projection_weight=projection_weight, adapter_down_maps=adapter_down_maps, adapter_up_maps=adapter_up_maps, prompt_token_length=prompt_token_length, prompt_of_request=prompt_of_request, adapter_of_request=adapter_of_request, adapter_slot_index=adapter_slot_index)


def request_table(prompt_of_request, adapter_of_request, adapter_slot_index, prompts, slots, loaded_adapters):
    n_req = prompt_of_request.shape[0]
    before = lax.optimization_barrier(jnp.sum((prompt_of_request[None, :] < prompt_of_request[:, None]).astype(jnp.int32), axis=1))
    position = jnp.arange(n_req, dtype=jnp.int32) - before
    adapter_hot = adapter_of_request[:, None] == jnp.arange(adapter_slot_index.shape[0], dtype=jnp.int32)[None, :]
    slot_index = lax.optimization_barrier(jnp.sum(jnp.where(adapter_hot, adapter_slot_index[None, :], 0), axis=1))
    prompt_hot = (prompt_of_request[:, None] == jnp.arange(prompts, dtype=jnp.int32)[None, :]).astype(jnp.float32)
    place_hot = (position[:, None] == jnp.arange(slots, dtype=jnp.int32)[None, :]).astype(jnp.float32)
    slot_hot = (slot_index[:, None] == jnp.arange(loaded_adapters, dtype=jnp.int32)[None, :]).astype(jnp.float32)
    paired = (place_hot[:, :, None] * slot_hot[:, None, :]).reshape(n_req, slots * loaded_adapters)
    return jnp.dot(prompt_hot.T, paired, precision=lax.Precision.HIGHEST)

def reference(prompt_token_states, gain, projection_weight, adapter_down_maps, adapter_up_maps, prompt_token_length, prompt_of_request, adapter_of_request, adapter_slot_index):
    states = prompt_token_states.astype(jnp.float32)
    scale_rows = lax.rsqrt(lax.optimization_barrier(jnp.mean(states * states, axis=1, keepdims=True)) + 1e-05)
    normalized_states = (states * scale_rows * gain.astype(jnp.float32)[None, :]).astype(jnp.bfloat16)
    base = jnp.dot(normalized_states, projection_weight.reshape(MODEL_WIDTH, 2 * MODEL_WIDTH), preferred_element_type=jnp.float32)
    low_rank_rows = jnp.einsum('bf,lfm->blm', normalized_states.astype(jnp.float32), adapter_down_maps.astype(jnp.float32)).astype(jnp.bfloat16)
    table = request_table(prompt_of_request, adapter_of_request, adapter_slot_index, PROMPTS, SLOTS, LIVE_ADAPTERS)
    ends = jnp.cumsum(prompt_token_length)
    token_index = jnp.arange(PTOK, dtype=jnp.int32)
    prompt_of = lax.optimization_barrier(jnp.sum((token_index[:, None] >= ends[None, :]).astype(jnp.int32), axis=1))
    prompt_hot = (prompt_of[:, None] == jnp.arange(PROMPTS, dtype=jnp.int32)[None, :]).astype(jnp.float32)
    pick = jnp.dot(prompt_hot, table, precision=lax.Precision.HIGHEST).reshape(PTOK, SLOTS, LIVE_ADAPTERS)
    adapter_up_weight = adapter_up_maps.astype(jnp.float32)
    block_rows = PTOK // N_COL

    def one_block(block):
        start = (block * block_rows).astype(jnp.int32)
        rank_block = lax.dynamic_slice_in_dim(low_rank_rows, start, block_rows, 0).astype(jnp.float32)
        rank_block = rank_block.reshape(block_rows, LIVE_ADAPTERS, 2, ADAPTER_RANK)
        delta = jnp.einsum('pqsm,qsmn->pqsn', rank_block, adapter_up_weight).astype(jnp.bfloat16)
        delta = delta.reshape(block_rows, LIVE_ADAPTERS, 2 * MODEL_WIDTH).astype(jnp.float32)
        pick_block = lax.dynamic_slice_in_dim(pick, start, block_rows, 0)
        base_block = lax.dynamic_slice_in_dim(base, start, block_rows, 0)
        live = lax.optimization_barrier(jnp.sum(pick_block, axis=2))
        mixed = live[:, :, None] * base_block[:, None, :] + jnp.einsum('tka,taf->tkf', pick_block, delta)
        return mixed.astype(jnp.bfloat16)
    mixed = lax.map(one_block, jnp.arange(N_COL, dtype=jnp.int32)).reshape(PTOK, SLOTS, 2 * MODEL_WIDTH)
    return (mixed[:, :, :MODEL_WIDTH], mixed[:, :, MODEL_WIDTH:])
```

```python
import functools

import jax
import jax.numpy as jnp
from jax import lax
from jax.experimental import pallas as pl
from jax.experimental.pallas import tpu as pltpu
from jax.sharding import PartitionSpec as P

SLOTS = 16
GROUP = 16


def mix_kernel(
    col_ref, rank_ref, up_ref, base_ref, scale_ref, pick_ref, out_ref, rows_ref, *, adapters, low_rank
):
    tokens = base_ref.shape[0]
    groups = tokens // GROUP
    used = adapters * GROUP
    col = col_ref[0]
    scale = scale_ref[...]

    @pl.when(pl.program_id(0) == 0)
    def _():
        rows_ref[:, used + 2 * GROUP :, :] = jnp.zeros_like(rows_ref[:, used + 2 * GROUP :, :])

    for a in range(adapters):
        delta = jnp.dot(
            rank_ref[lax.bitwise_xor(col, a), 0], up_ref[a, 0], preferred_element_type=jnp.float32
        )
        delta = (delta * scale).astype(jnp.bfloat16)
        for g in range(groups):
            rows_ref[g, a * GROUP : (a + 1) * GROUP, :] = delta[g * GROUP : (g + 1) * GROUP, :]
    base = base_ref[...] * scale
    high = base.astype(jnp.bfloat16)
    low = (base - high.astype(jnp.float32)).astype(jnp.bfloat16)
    for g in range(groups):
        rows_ref[g, used : used + GROUP, :] = high[g * GROUP : (g + 1) * GROUP, :]
        rows_ref[g, used + GROUP : used + 2 * GROUP, :] = low[g * GROUP : (g + 1) * GROUP, :]
    for g in range(groups):
        mixed = jnp.dot(pick_ref[g], rows_ref[g], preferred_element_type=jnp.float32)
        out_ref[g] = mixed.astype(jnp.bfloat16)


def mix(col, rank, up, base, scale, pick, half):
    adapters, _, tokens, low_rank = rank.shape
    width = up.shape[3]
    groups, rows, depth = pick.shape
    block = 256 if width % 256 == 0 else 128
    steps = width // block
    out = pl.pallas_call(
        functools.partial(mix_kernel, adapters=adapters, low_rank=low_rank),
        grid_spec=pltpu.PrefetchScalarGridSpec(
            num_scalar_prefetch=1,
            grid=(steps,),
            in_specs=[
                pl.BlockSpec((adapters, 1, tokens, low_rank), lambda i, _: (0, half, 0, 0)),
                pl.BlockSpec((adapters, 1, low_rank, block), lambda i, _: (0, half, 0, i)),
                pl.BlockSpec((tokens, block), lambda i, _: (0, half * steps + i)),
                pl.BlockSpec((tokens, 1), lambda i, _: (0, 0)),
                pl.BlockSpec((groups, rows, depth), lambda i, _: (0, 0, 0)),
            ],
            out_specs=pl.BlockSpec((groups, rows, block), lambda i, _: (0, 0, i)),
            scratch_shapes=[pltpu.VMEM((groups, depth, block), jnp.bfloat16)],
        ),
        out_shape=jax.ShapeDtypeStruct((groups, rows, width), jnp.bfloat16),
        compiler_params=pltpu.CompilerParams(vmem_limit_bytes=40 * 1024 * 1024),
        cost_estimate=pl.CostEstimate(
            flops=2 * groups * rows * depth * width,
            bytes_accessed=2 * groups * rows * width + 2 * adapters * low_rank * width,
            transcendentals=0,
        ),
    )(col, rank, up, base, scale, pick)
    return out.reshape(tokens, SLOTS, width)


def pick_matrix(
    token_index,
    prompt_token_length,
    prompt_of_request,
    adapter_of_request,
    adapter_slot_index,
    adapters,
    depth,
):
    tokens = token_index.shape[0]
    ends = jnp.cumsum(prompt_token_length)
    prompt_of = jnp.sum((token_index[:, None] >= ends[None, :]).astype(jnp.int32), axis=1)
    first = jnp.sum((prompt_of_request[None, :] < prompt_of[:, None]).astype(jnp.int32), axis=1)
    after = jnp.sum((prompt_of_request[None, :] <= prompt_of[:, None]).astype(jnp.int32), axis=1)
    hot = adapter_of_request[:, None] == jnp.arange(adapter_slot_index.shape[0], dtype=jnp.int32)[None, :]
    slot_of = jnp.sum(jnp.where(hot, adapter_slot_index[None, :], 0), axis=1)
    request = first[:, None] + jnp.arange(SLOTS, dtype=jnp.int32)[None, :]
    live = request < after[:, None]
    requests = jnp.arange(prompt_of_request.shape[0], dtype=jnp.int32)
    slot = jnp.sum(
        jnp.where(request[:, :, None] == requests[None, None, :], slot_of[None, None, :], 0), axis=2
    )
    place = (jnp.arange(tokens, dtype=jnp.int32) % GROUP)[:, None]
    column = jnp.where(live, slot * GROUP + place, -1)
    columns = jnp.arange(depth, dtype=jnp.int32)[None, None, :]
    used = adapters * GROUP
    of_base = (columns >= used) & (columns < used + 2 * GROUP) & (columns % GROUP == place[:, :, None])
    pick = (columns == column[:, :, None]) | (of_base & live[:, :, None])
    return pick.astype(jnp.bfloat16).reshape(tokens // GROUP, GROUP * SLOTS, depth)


def body(
    prompt_token_states,
    gain,
    projection_weight,
    adapter_down_maps,
    adapter_up_maps,
    prompt_token_length,
    prompt_of_request,
    adapter_of_request,
    adapter_slot_index,
):
    rows, cols = lax.axis_size("row"), lax.axis_size("col")
    row, col = lax.axis_index("row"), lax.axis_index("col")
    lines = cols // 2
    line, side = col // 2, col % 2
    tokens, width = prompt_token_states.shape
    depth_in = projection_weight.shape[0]
    low_rank = adapter_down_maps.shape[2] // 2
    adapters = cols

    def send(value, pairs):
        flat = [(a * cols + b, c * cols + d) for (a, b), (c, d) in pairs]
        return lax.ppermute(value, ("row", "col"), flat)

    every = [(r, c) for r in range(rows) for c in range(cols)]

    def to_side(value):
        return send(value, [((r, c), (r, c ^ 1)) for r, c in every])

    def to_line(value, k):
        return send(value, [((r, c), (r, c ^ (2 * k))) for r, c in every])

    def to_owner(value, k):
        return send(
            value, [((r, 2 * (r ^ k) + s), (r, 2 * r + s)) for r in range(rows) for s in range(2)]
        )

    def over_rows(value):
        bit = 2
        while bit < rows:
            got = send(
                value,
                [
                    ((c // 2 ^ e, c), (c // 2 ^ e ^ bit, c))
                    for c in range(cols)
                    for e in range(0, bit, 2)
                ],
            )
            value = jnp.where((row ^ line) & bit != 0, got, value)
            bit *= 2
        got = send(value, [((c // 2 ^ e, c), (c // 2 ^ e ^ 1, c)) for c in range(cols) for e in range(0, rows, 2)])
        return jnp.where((row ^ line) & 1 != 0, got, value)

    up = lax.all_gather(adapter_up_maps, "col", axis=0, tiled=True)

    states = prompt_token_states.astype(jnp.float32)
    gained = (states * gain.astype(jnp.float32)[None, :]).astype(jnp.bfloat16)
    mine = lax.dynamic_slice_in_dim(gained, side * depth_in, depth_in, 1)
    theirs = lax.dynamic_slice_in_dim(gained, (1 - side) * depth_in, depth_in, 1)
    block = jnp.stack([mine, to_side(theirs)])
    other_down = to_side(adapter_down_maps[0])
    blocks = [over_rows(block)] + [over_rows(to_owner(block, k)) for k in range(1, lines)]

    weight = projection_weight.reshape(depth_in, 2 * width)
    sums = []
    for k in range(lines):
        out = jnp.dot(blocks[k][1], weight, preferred_element_type=jnp.float32).astype(jnp.bfloat16)
        kept = jnp.dot(blocks[k][0], weight, preferred_element_type=jnp.float32)
        sums.append(kept + to_side(out).astype(jnp.float32))
    base = sums[0]
    for k in range(1, lines):
        base = base + to_line(sums[k].astype(jnp.bfloat16), k).astype(jnp.float32)

    gathered = jnp.concatenate([gained] + [to_line(gained, k) for k in range(1, lines)], axis=0)
    down = jnp.concatenate([adapter_down_maps[0], other_down], axis=1)
    partial = jnp.dot(gathered, down, preferred_element_type=jnp.float32)
    partial = partial.reshape(lines, tokens, 4 * low_rank)
    held = lax.dynamic_index_in_dim(partial, row ^ line, 0, keepdims=False)
    for j in range(1, rows):
        out = lax.dynamic_index_in_dim(partial, row ^ j ^ line, 0, keepdims=False)
        held = held + send(out, [((r, c), (r ^ j, c)) for r, c in every])
    held = held.astype(jnp.bfloat16)
    ranks = jnp.stack([held] + [to_owner(held, k) for k in range(1, lines)])
    ranks = over_rows(ranks)
    ranks = ranks.reshape(lines, tokens, 2, 2, low_rank).transpose(0, 2, 3, 1, 4)
    ranks = ranks.reshape(adapters, 2, tokens, low_rank)

    square_sum = lax.psum(jnp.sum(states * states, axis=1), "row")
    scale = lax.rsqrt(square_sum / (width * rows) + 1e-05)[:, None]
    depth = -(-(adapters * GROUP + 2 * GROUP) // 128) * 128
    token_index = col * tokens + jnp.arange(tokens, dtype=jnp.int32)
    pick = pick_matrix(
        token_index,
        prompt_token_length,
        prompt_of_request,
        adapter_of_request,
        adapter_slot_index,
        adapters,
        depth,
    )
    place = col.astype(jnp.int32).reshape(1)
    return tuple(mix(place, ranks, up, base, scale, pick, half) for half in range(2))


def solution(mesh):
    placed = (
        P("col", "row"),
        P("row"),
        P("col", None, "row"),
        P("col", "row", None),
        P("col", None, None, "row"),
        P(),
        P(),
        P(),
        P(),
    )
    return jax.shard_map(
        body,
        mesh=mesh,
        in_specs=placed,
        out_specs=(P("col", None, "row"), P("col", None, "row")),
        check_vma=False,
    )
```

```python
import functools

import jax
import jax.numpy as jnp
from jax import lax
from jax.experimental import pallas as pl
from jax.experimental.pallas import tpu as pltpu
from jax.sharding import PartitionSpec as P

SLOTS = 16
GROUP = 16


def delta_kernel(rank_ref, up_ref, scale_ref, out_ref):
    product = jnp.dot(rank_ref[0], up_ref[0], preferred_element_type=jnp.float32)
    out_ref[...] = (product * scale_ref[...]).astype(jnp.bfloat16)


def corrections(rank, up, scale):
    _, tokens, low_rank = rank.shape
    width = up.shape[2]
    return pl.pallas_call(
        delta_kernel,
        grid=(2,),
        in_specs=[
            pl.BlockSpec((1, tokens, low_rank), lambda j: (j, 0, 0)),
            pl.BlockSpec((1, low_rank, width), lambda j: (j, 0, 0)),
            pl.BlockSpec((tokens, 1), lambda j: (0, 0)),
        ],
        out_specs=pl.BlockSpec((tokens, width), lambda j: (0, j)),
        out_shape=jax.ShapeDtypeStruct((tokens, 2 * width), jnp.bfloat16),
        compiler_params=pltpu.CompilerParams(vmem_limit_bytes=24 * 1024 * 1024),
        cost_estimate=pl.CostEstimate(
            flops=4 * tokens * low_rank * width,
            bytes_accessed=4 * (tokens * width + low_rank * width),
            transcendentals=0,
        ),
    )(rank, up, scale)


def mix_kernel(*refs, adapters, parts):
    deltas, bases = refs[:adapters], refs[adapters : adapters + parts]
    scale_ref, pick_ref, out_ref, rows_ref = refs[adapters + parts :]
    tokens = scale_ref.shape[0]
    groups = tokens // GROUP
    used = adapters * GROUP

    @pl.when(pl.program_id(0) == 0)
    def _():
        rows_ref[:, used + 2 * GROUP :, :] = jnp.zeros_like(rows_ref[:, used + 2 * GROUP :, :])

    base = bases[0][...].astype(jnp.float32)
    for part in bases[1:]:
        base = base + part[...].astype(jnp.float32)
    base = base * scale_ref[...]
    high = base.astype(jnp.bfloat16)
    low = (base - high.astype(jnp.float32)).astype(jnp.bfloat16)
    for g in range(groups):
        here = slice(g * GROUP, (g + 1) * GROUP)
        for a in range(adapters):
            rows_ref[g, a * GROUP : (a + 1) * GROUP, :] = deltas[a][here, :]
        rows_ref[g, used : used + GROUP, :] = high[here, :]
        rows_ref[g, used + GROUP : used + 2 * GROUP, :] = low[here, :]
    for g in range(groups):
        mixed = jnp.dot(pick_ref[g], rows_ref[g], preferred_element_type=jnp.float32)
        out_ref[g] = mixed.astype(jnp.bfloat16)


def mix(deltas, bases, scale, pick, half):
    tokens, width = deltas[0].shape[0], deltas[0].shape[1] // 2
    groups, rows, depth = pick.shape
    block = 256 if width % 256 == 0 else 128
    steps = width // block
    column = pl.BlockSpec((tokens, block), lambda i: (0, half * steps + i))
    out = pl.pallas_call(
        functools.partial(mix_kernel, adapters=len(deltas), parts=len(bases)),
        grid=(steps,),
        in_specs=[column] * (len(deltas) + len(bases))
        + [
            pl.BlockSpec((tokens, 1), lambda i: (0, 0)),
            pl.BlockSpec((groups, rows, depth), lambda i: (0, 0, 0)),
        ],
        out_specs=pl.BlockSpec((groups, rows, block), lambda i: (0, 0, i)),
        scratch_shapes=[pltpu.VMEM((groups, depth, block), jnp.bfloat16)],
        out_shape=jax.ShapeDtypeStruct((groups, rows, width), jnp.bfloat16),
        compiler_params=pltpu.CompilerParams(vmem_limit_bytes=40 * 1024 * 1024),
        cost_estimate=pl.CostEstimate(
            flops=2 * groups * rows * depth * width,
            bytes_accessed=2 * groups * rows * width,
            transcendentals=0,
        ),
    )(*deltas, *bases, scale, pick)
    return out.reshape(tokens, SLOTS, width)


def pick_matrix(
    token_index,
    prompt_token_length,
    prompt_of_request,
    adapter_of_request,
    adapter_slot_index,
    adapters,
    depth,
    order,
):
    tokens = token_index.shape[0]
    ends = jnp.cumsum(prompt_token_length)
    prompt_of = jnp.sum((token_index[:, None] >= ends[None, :]).astype(jnp.int32), axis=1)
    first = jnp.sum((prompt_of_request[None, :] < prompt_of[:, None]).astype(jnp.int32), axis=1)
    after = jnp.sum((prompt_of_request[None, :] <= prompt_of[:, None]).astype(jnp.int32), axis=1)
    hot = adapter_of_request[:, None] == jnp.arange(adapter_slot_index.shape[0], dtype=jnp.int32)[None, :]
    slot_of = jnp.sum(jnp.where(hot, adapter_slot_index[None, :], 0), axis=1)
    request = first[:, None] + jnp.arange(SLOTS, dtype=jnp.int32)[None, :]
    live = request < after[:, None]
    requests = jnp.arange(prompt_of_request.shape[0], dtype=jnp.int32)
    slot = jnp.sum(
        jnp.where(request[:, :, None] == requests[None, None, :], slot_of[None, None, :], 0), axis=2
    )
    place = (jnp.arange(tokens, dtype=jnp.int32) % GROUP)[:, None]
    column = jnp.where(live, order(slot) * GROUP + place, -1)
    columns = jnp.arange(depth, dtype=jnp.int32)[None, None, :]
    used = adapters * GROUP
    of_base = (columns >= used) & (columns < used + 2 * GROUP) & (columns % GROUP == place[:, :, None])
    pick = (columns == column[:, :, None]) | (of_base & live[:, :, None])
    return pick.astype(jnp.bfloat16).reshape(tokens // GROUP, GROUP * SLOTS, depth)


def body(
    prompt_token_states,
    gain,
    projection_weight,
    adapter_down_maps,
    adapter_up_maps,
    prompt_token_length,
    prompt_of_request,
    adapter_of_request,
    adapter_slot_index,
):
    rows, cols = lax.axis_size("row"), lax.axis_size("col")
    row, col = lax.axis_index("row"), lax.axis_index("col")
    lines = cols // 2
    line, side = col // 2, col % 2
    tokens, width = prompt_token_states.shape
    depth_in = projection_weight.shape[0]
    low_rank = adapter_down_maps.shape[2] // 2
    adapters = cols

    def send(value, pairs):
        flat = [(a * cols + b, c * cols + d) for (a, b), (c, d) in pairs]
        return lax.ppermute(value, ("row", "col"), flat)

    every = [(r, c) for r in range(rows) for c in range(cols)]

    def to_side(value):
        return send(value, [((r, c), (r, c ^ 1)) for r, c in every])

    def to_line(value, k):
        return send(value, [((r, c), (r, c ^ (2 * k))) for r, c in every])

    def to_owner(value, k):
        return send(
            value, [((r, 2 * (r ^ k) + s), (r, 2 * r + s)) for r in range(rows) for s in range(2)]
        )

    def over_rows(value, *before_last):
        bit = 2
        while bit < rows:
            got = send(
                value,
                [
                    ((c // 2 ^ e, c), (c // 2 ^ e ^ bit, c))
                    for c in range(cols)
                    for e in range(0, bit, 2)
                ],
            )
            value = jnp.where((row ^ line) & bit != 0, got, value)
            bit *= 2
        if before_last:
            value = lax.optimization_barrier((value, *before_last))[0]
        got = send(
            value,
            [((c // 2 ^ e, c), (c // 2 ^ e ^ 1, c)) for c in range(cols) for e in range(0, rows, 2)],
        )
        return jnp.where((row ^ line) & 1 != 0, got, value)

    def after(value, *others):
        return lax.optimization_barrier((value, *others))[0]

    def pairs_of(lines_pairs):
        return [
            ((r, 2 * a + s), (r, 2 * b + s)) for r in range(rows) for a, b in lines_pairs for s in range(2)
        ]

    across = pairs_of([(1, 2), (2, 1)])
    outward = pairs_of([(1, 0), (2, 3)])
    inner = (line == 1) | (line == 2)
    up_own = adapter_up_maps[0]
    weight = projection_weight.reshape(depth_in, 2 * width)

    states = prompt_token_states.astype(jnp.float32)
    gained = (states * gain.astype(jnp.float32)[None, :]).astype(jnp.bfloat16)

    def halves(values):
        mine = lax.dynamic_slice_in_dim(values, side * depth_in, depth_in, 2)
        theirs = lax.dynamic_slice_in_dim(values, (1 - side) * depth_in, depth_in, 2)
        return mine, send(theirs, [((c // 2, c), (c // 2, c ^ 1)) for c in range(cols)])

    def product(value):
        return jnp.dot(value, weight, preferred_element_type=jnp.float32)

    rest = [to_line(gained, k) for k in range(1, lines)]
    both = over_rows(jnp.stack(halves(gained[None])))
    other_down = to_side(after(adapter_down_maps[0], gained))
    up_other = to_side(after(up_own, gained))
    own_out = to_side(product(both[1, 0]).astype(jnp.bfloat16))
    own_kept = product(both[0, 0])

    late = lax.optimization_barrier((up_own, *rest))
    up_late, rest = late[0], late[1:]
    if lines == 4:
        near = to_line(up_late, 1)
        far_near = send(up_late, across)
    else:
        near = to_line(up_late, 1)
        far_near = near

    mine, got = halves(jnp.stack(rest))
    gathered = jnp.concatenate([gained, *rest], axis=0)
    gathered, other_down, up_other = lax.optimization_barrier((gathered, other_down, up_other))
    down = jnp.concatenate([adapter_down_maps[0], other_down], axis=1)
    partial = jnp.dot(gathered, down, preferred_element_type=jnp.float32)
    got, partial = lax.optimization_barrier((got, partial))
    partial = partial.reshape(lines, tokens, 4 * low_rank)
    parts = {
        m: lax.dynamic_index_in_dim(partial, row ^ line ^ m, 0, keepdims=False) for m in range(rows)
    }
    bit = 1
    while bit < rows:
        leaving = [m for m in parts if m & bit]
        arrived = send(
            jnp.stack([parts.pop(m) for m in leaving]), [((r, c), (r ^ bit, c)) for r, c in every]
        )
        for i, m in enumerate(leaving):
            parts[m ^ bit] = parts[m ^ bit] + arrived[i]
        bit *= 2
    held = parts[0].astype(jnp.bfloat16)

    both = over_rows(jnp.stack([mine, got]), held, near, far_near)
    both = after(both, own_out)
    outs = [product(both[1, k]).astype(jnp.bfloat16) for k in range(lines - 1)]
    kept = [product(both[0, k]) for k in range(lines - 1)]
    came = [None] * (lines - 1)
    for k in reversed(range(lines - 1)):
        came[k] = to_side(outs[k])

    ranks = [held] + [to_owner(held, k) for k in range(1, lines)]
    if lines == 4:
        far_far = send(near, across)
        first = send(far_near, outward)
        far_far, first, *ranks = lax.optimization_barrier((far_far, first, *ranks, came[-1]))[:-1]
        last = jnp.where(inner, far_far, send(far_far, outward))
        first = jnp.where(inner, far_near, first)
        blocks = [near, first, last]
    else:
        blocks = [near] + [to_line(up_own, k) for k in range(2, lines)]
    ranks = over_rows(jnp.stack(ranks))
    ranks = ranks.reshape(lines, tokens, 2, 2, low_rank).transpose(0, 2, 3, 1, 4)
    ranks = ranks.reshape(adapters, 2, tokens, low_rank)
    if lines == 4:
        far = jnp.where(inner, jnp.concatenate([ranks[6:], ranks[4:6]]), ranks[4:])
        ranks = jnp.concatenate([ranks[:4], far])

    ups = [up_own, up_other]
    for value in blocks:
        ups += [value, to_side(after(value, came[-1]))]

    bases = [own_kept + own_out.astype(jnp.float32)]
    for k in reversed(range(lines - 1)):
        total = kept[k] + came[k].astype(jnp.float32)
        bases.append(to_line(total.astype(jnp.bfloat16), k + 1))

    def order(slot):
        place = slot ^ col
        return jnp.where(inner & (place >= 4), place ^ 2, place) if lines == 4 else place

    square_sum = after(jnp.sum(states * states, axis=1), partial)
    total = square_sum
    for j in range(1, rows):
        total = total + send(square_sum, [((r, c), (r ^ j, c)) for r, c in every])
    scale = lax.rsqrt(total / (width * rows) + 1e-05)[:, None]
    depth = -(-(adapters * GROUP + 2 * GROUP) // 128) * 128
    token_index = col * tokens + jnp.arange(tokens, dtype=jnp.int32)
    pick = pick_matrix(
        token_index,
        prompt_token_length,
        prompt_of_request,
        adapter_of_request,
        adapter_slot_index,
        adapters,
        depth,
        order,
    )
    deltas = [corrections(ranks[e], ups[e], scale) for e in range(adapters)]
    return tuple(mix(deltas, bases, scale, pick, half) for half in range(2))


def solution(mesh):
    placed = (
        P("col", "row"),
        P("row"),
        P("col", None, "row"),
        P("col", "row", None),
        P("col", None, None, "row"),
        P(),
        P(),
        P(),
        P(),
    )
    return jax.shard_map(
        body,
        mesh=mesh,
        in_specs=placed,
        out_specs=(P("col", None, "row"), P("col", None, "row")),
        check_vma=False,
    )
```

```python
import functools

import jax
import jax.numpy as jnp
from jax import lax
from jax.experimental import pallas as pl
from jax.experimental.pallas import tpu as pltpu
from jax.sharding import PartitionSpec as P

SLOTS = 16
GROUP = 16


def delta_kernel(rank_ref, up_ref, scale_ref, out_ref):
    product = jnp.dot(rank_ref[0], up_ref[0], preferred_element_type=jnp.float32)
    out_ref[...] = (product * scale_ref[...]).astype(jnp.bfloat16)


def corrections(rank, up, scale):
    _, tokens, low_rank = rank.shape
    width = up.shape[2]
    return pl.pallas_call(
        delta_kernel,
        grid=(2,),
        in_specs=[
            pl.BlockSpec((1, tokens, low_rank), lambda j: (j, 0, 0)),
            pl.BlockSpec((1, low_rank, width), lambda j: (j, 0, 0)),
            pl.BlockSpec((tokens, 1), lambda j: (0, 0)),
        ],
        out_specs=pl.BlockSpec((tokens, width), lambda j: (0, j)),
        out_shape=jax.ShapeDtypeStruct((tokens, 2 * width), jnp.bfloat16),
        compiler_params=pltpu.CompilerParams(vmem_limit_bytes=24 * 1024 * 1024),
        cost_estimate=pl.CostEstimate(
            flops=4 * tokens * low_rank * width,
            bytes_accessed=4 * (tokens * width + low_rank * width),
            transcendentals=0,
        ),
    )(rank, up, scale)


def mix_kernel(*refs, adapters, parts):
    deltas, bases = refs[:adapters], refs[adapters : adapters + parts]
    scale_ref, pick_ref, out_ref, rows_ref = refs[adapters + parts :]
    tokens = scale_ref.shape[0]
    groups = tokens // GROUP
    used = adapters * GROUP

    @pl.when(pl.program_id(0) == 0)
    def _():
        rows_ref[:, used + 2 * GROUP :, :] = jnp.zeros_like(rows_ref[:, used + 2 * GROUP :, :])

    base = bases[0][...].astype(jnp.float32)
    for part in bases[1:]:
        base = base + part[...].astype(jnp.float32)
    base = base * scale_ref[...]
    high = base.astype(jnp.bfloat16)
    low = (base - high.astype(jnp.float32)).astype(jnp.bfloat16)
    for g in range(groups):
        here = slice(g * GROUP, (g + 1) * GROUP)
        for a in range(adapters):
            rows_ref[g, a * GROUP : (a + 1) * GROUP, :] = deltas[a][here, :]
        rows_ref[g, used : used + GROUP, :] = high[here, :]
        rows_ref[g, used + GROUP : used + 2 * GROUP, :] = low[here, :]
    for g in range(groups):
        mixed = jnp.dot(pick_ref[g], rows_ref[g], preferred_element_type=jnp.float32)
        out_ref[g] = mixed.astype(jnp.bfloat16)


def mix(deltas, bases, scale, pick, half):
    tokens, width = deltas[0].shape[0], deltas[0].shape[1] // 2
    groups, rows, depth = pick.shape
    block = next(n for n in (640, 256, 128) if width % n == 0)
    steps = width // block
    column = pl.BlockSpec((tokens, block), lambda i: (0, half * steps + i))
    out = pl.pallas_call(
        functools.partial(mix_kernel, adapters=len(deltas), parts=len(bases)),
        grid=(steps,),
        in_specs=[column] * (len(deltas) + len(bases))
        + [
            pl.BlockSpec((tokens, 1), lambda i: (0, 0)),
            pl.BlockSpec((groups, rows, depth), lambda i: (0, 0, 0)),
        ],
        out_specs=pl.BlockSpec((groups, rows, block), lambda i: (0, 0, i)),
        scratch_shapes=[pltpu.VMEM((groups, depth, block), jnp.bfloat16)],
        out_shape=jax.ShapeDtypeStruct((groups, rows, width), jnp.bfloat16),
        compiler_params=pltpu.CompilerParams(vmem_limit_bytes=40 * 1024 * 1024),
        cost_estimate=pl.CostEstimate(
            flops=2 * groups * rows * depth * width,
            bytes_accessed=2 * groups * rows * width,
            transcendentals=0,
        ),
    )(*deltas, *bases, scale, pick)
    return out.reshape(tokens, SLOTS, width)


def pick_matrix(
    token_index,
    prompt_token_length,
    prompt_of_request,
    adapter_of_request,
    adapter_slot_index,
    adapters,
    depth,
    order,
):
    tokens = token_index.shape[0]
    ends = jnp.cumsum(prompt_token_length)
    prompt_of = jnp.sum((token_index[:, None] >= ends[None, :]).astype(jnp.int32), axis=1)
    first = jnp.sum((prompt_of_request[None, :] < prompt_of[:, None]).astype(jnp.int32), axis=1)
    after = jnp.sum((prompt_of_request[None, :] <= prompt_of[:, None]).astype(jnp.int32), axis=1)
    hot = adapter_of_request[:, None] == jnp.arange(adapter_slot_index.shape[0], dtype=jnp.int32)[None, :]
    slot_of = jnp.sum(jnp.where(hot, adapter_slot_index[None, :], 0), axis=1)
    request = first[:, None] + jnp.arange(SLOTS, dtype=jnp.int32)[None, :]
    live = request < after[:, None]
    requests = jnp.arange(prompt_of_request.shape[0], dtype=jnp.int32)
    slot = jnp.sum(
        jnp.where(request[:, :, None] == requests[None, None, :], slot_of[None, None, :], 0), axis=2
    )
    place = (jnp.arange(tokens, dtype=jnp.int32) % GROUP)[:, None]
    column = jnp.where(live, order(slot) * GROUP + place, -1)
    columns = jnp.arange(depth, dtype=jnp.int32)[None, None, :]
    used = adapters * GROUP
    of_base = (columns >= used) & (columns < used + 2 * GROUP) & (columns % GROUP == place[:, :, None])
    pick = (columns == column[:, :, None]) | (of_base & live[:, :, None])
    return pick.astype(jnp.bfloat16).reshape(tokens // GROUP, GROUP * SLOTS, depth)


def body(
    prompt_token_states,
    gain,
    projection_weight,
    adapter_down_maps,
    adapter_up_maps,
    prompt_token_length,
    prompt_of_request,
    adapter_of_request,
    adapter_slot_index,
):
    rows, cols = lax.axis_size("row"), lax.axis_size("col")
    row, col = lax.axis_index("row"), lax.axis_index("col")
    lines = cols // 2
    line, side = col // 2, col % 2
    tokens, width = prompt_token_states.shape
    depth_in = projection_weight.shape[0]
    low_rank = adapter_down_maps.shape[2] // 2
    adapters = cols

    def send(value, pairs):
        flat = [(a * cols + b, c * cols + d) for (a, b), (c, d) in pairs]
        return lax.ppermute(value, ("row", "col"), flat)

    every = [(r, c) for r in range(rows) for c in range(cols)]

    def to_side(value):
        return send(value, [((r, c), (r, c ^ 1)) for r, c in every])

    def to_line(value, k):
        return send(value, [((r, c), (r, c ^ (2 * k))) for r, c in every])

    def to_owner(value, k):
        return send(
            value, [((r, 2 * (r ^ k) + s), (r, 2 * r + s)) for r in range(rows) for s in range(2)]
        )

    def over_rows(value, *before_last):
        bit = 2
        while bit < rows:
            got = send(
                value,
                [
                    ((c // 2 ^ e, c), (c // 2 ^ e ^ bit, c))
                    for c in range(cols)
                    for e in range(0, bit, 2)
                ],
            )
            value = jnp.where((row ^ line) & bit != 0, got, value)
            bit *= 2
        if before_last:
            value = lax.optimization_barrier((value, *before_last))[0]
        got = send(
            value,
            [((c // 2 ^ e, c), (c // 2 ^ e ^ 1, c)) for c in range(cols) for e in range(0, rows, 2)],
        )
        return jnp.where((row ^ line) & 1 != 0, got, value)

    def after(value, *others):
        return lax.optimization_barrier((value, *others))[0]

    def pairs_of(lines_pairs):
        return [
            ((r, 2 * a + s), (r, 2 * b + s)) for r in range(rows) for a, b in lines_pairs for s in range(2)
        ]

    across = pairs_of([(1, 2), (2, 1)])
    outward = pairs_of([(1, 0), (2, 3)])
    inner = (line == 1) | (line == 2)
    up_own = adapter_up_maps[0]
    weight = projection_weight.reshape(depth_in, 2 * width)

    states = prompt_token_states.astype(jnp.float32)
    gained = (states * gain.astype(jnp.float32)[None, :]).astype(jnp.bfloat16)

    def halves(values):
        mine = lax.dynamic_slice_in_dim(values, side * depth_in, depth_in, 2)
        theirs = lax.dynamic_slice_in_dim(values, (1 - side) * depth_in, depth_in, 2)
        return mine, send(theirs, [((c // 2, c), (c // 2, c ^ 1)) for c in range(cols)])

    def product(value):
        return jnp.dot(value, weight, preferred_element_type=jnp.float32)

    rest = [to_line(gained, k) for k in range(1, lines)]
    both = over_rows(jnp.stack(halves(gained[None])))
    other_down = to_side(after(adapter_down_maps[0], gained))
    up_other = to_side(after(up_own, gained))
    own_out = to_side(product(both[1, 0]).astype(jnp.bfloat16))
    own_kept = product(both[0, 0])

    late = lax.optimization_barrier((up_own, *rest))
    up_late, rest = late[0], late[1:]
    if lines == 4:
        near = to_line(jnp.stack([up_late, up_other]), 1)
        near, near_other = near[0], near[1]
        far_near = send(up_late, across)
    else:
        near = to_line(up_late, 1)
        far_near = near

    mine, got = halves(jnp.stack(rest))
    gathered = jnp.concatenate([gained, *rest], axis=0)
    gathered, other_down, up_other = lax.optimization_barrier((gathered, other_down, up_other))
    down = jnp.concatenate([adapter_down_maps[0], other_down], axis=1)
    partial = jnp.dot(gathered, down, preferred_element_type=jnp.float32)
    got, partial = lax.optimization_barrier((got, partial))
    partial = partial.reshape(lines, tokens, 4 * low_rank)
    parts = {
        m: lax.dynamic_index_in_dim(partial, row ^ line ^ m, 0, keepdims=False) for m in range(rows)
    }
    bit = 1
    while bit < rows:
        leaving = [m for m in parts if m & bit]
        arrived = send(
            jnp.stack([parts.pop(m) for m in leaving]), [((r, c), (r ^ bit, c)) for r, c in every]
        )
        for i, m in enumerate(leaving):
            parts[m ^ bit] = parts[m ^ bit] + arrived[i]
        bit *= 2
    held = parts[0].astype(jnp.bfloat16)

    both = over_rows(jnp.stack([mine, got]), held)
    both = after(both, own_out)
    outs = [product(both[1, k]).astype(jnp.bfloat16) for k in range(lines - 1)]
    kept = [product(both[0, k]) for k in range(lines - 1)]
    came = [None] * (lines - 1)
    for k in reversed(range(lines - 1)):
        came[k] = to_side(outs[k])

    ranks = [held] + [to_owner(held, k) for k in range(1, lines)]
    if lines == 4:
        far_far = send(near, across)
        first = send(far_near, outward)
        far_far, first, *ranks = lax.optimization_barrier((far_far, first, *ranks, came[-1]))[:-1]
        last = jnp.where(inner, far_far, send(far_far, outward))
        first = jnp.where(inner, far_near, first)
        blocks = [first, last]
        ups = [up_own, up_other, near, near_other]
    else:
        blocks = [near] + [to_line(up_own, k) for k in range(2, lines)]
        ups = [up_own, up_other]
    ranks = over_rows(jnp.stack(ranks))
    ranks = ranks.reshape(lines, tokens, 2, 2, low_rank).transpose(0, 2, 3, 1, 4)
    ranks = ranks.reshape(adapters, 2, tokens, low_rank)
    if lines == 4:
        far = jnp.where(inner, jnp.concatenate([ranks[6:], ranks[4:6]]), ranks[4:])
        ranks = jnp.concatenate([ranks[:4], far])

    for value in blocks:
        ups += [value, to_side(after(value, came[-1]))]

    bases = [own_kept + own_out.astype(jnp.float32)]
    for k in reversed(range(lines - 1)):
        total = kept[k] + came[k].astype(jnp.float32)
        bases.append(to_line(total.astype(jnp.bfloat16), k + 1))

    def order(slot):
        place = slot ^ col
        return jnp.where(inner & (place >= 4), place ^ 2, place) if lines == 4 else place

    square_sum = after(jnp.sum(states * states, axis=1), partial)
    total = square_sum
    for j in range(1, rows):
        total = total + send(square_sum, [((r, c), (r ^ j, c)) for r, c in every])
    scale = lax.rsqrt(total / (width * rows) + 1e-05)[:, None]
    depth = -(-(adapters * GROUP + 2 * GROUP) // 128) * 128
    token_index = col * tokens + jnp.arange(tokens, dtype=jnp.int32)
    pick = pick_matrix(
        token_index,
        prompt_token_length,
        prompt_of_request,
        adapter_of_request,
        adapter_slot_index,
        adapters,
        depth,
        order,
    )
    deltas = [corrections(ranks[e], ups[e], scale) for e in range(adapters)]
    return tuple(mix(deltas, bases, scale, pick, half) for half in range(2))


def solution(mesh):
    placed = (
        P("col", "row"),
        P("row"),
        P("col", None, "row"),
        P("col", "row", None),
        P("col", None, None, "row"),
        P(),
        P(),
        P(),
        P(),
    )
    return jax.shard_map(
        body,
        mesh=mesh,
        in_specs=placed,
        out_specs=(P("col", None, "row"), P("col", None, "row")),
        check_vma=False,
    )
```

```python
import functools

import jax
import jax.numpy as jnp
from jax import lax
from jax.experimental import pallas as pl
from jax.experimental.pallas import tpu as pltpu
from jax.sharding import PartitionSpec as P

SLOTS = 16
GROUP = 16


def delta_kernel(rank_ref, up_ref, scale_ref, out_ref):
    product = jnp.dot(rank_ref[0], up_ref[0], preferred_element_type=jnp.float32)
    out_ref[...] = (product * scale_ref[...]).astype(jnp.bfloat16)


def corrections(rank, up, scale):
    _, tokens, low_rank = rank.shape
    n, _, width = up.shape
    return pl.pallas_call(
        delta_kernel,
        grid=(n,),
        in_specs=[
            pl.BlockSpec((1, tokens, low_rank), lambda j: (j, 0, 0)),
            pl.BlockSpec((1, low_rank, width), lambda j: (j, 0, 0)),
            pl.BlockSpec((tokens, 1), lambda j: (0, 0)),
        ],
        out_specs=pl.BlockSpec((tokens, width), lambda j: (0, j)),
        out_shape=jax.ShapeDtypeStruct((tokens, n * width), jnp.bfloat16),
        compiler_params=pltpu.CompilerParams(vmem_limit_bytes=24 * 1024 * 1024),
        cost_estimate=pl.CostEstimate(
            flops=2 * n * tokens * low_rank * width,
            bytes_accessed=2 * n * (tokens * width + low_rank * width),
            transcendentals=0,
        ),
    )(rank, up, scale)


def mix_kernel(*refs, adapters, parts):
    deltas, bases = refs[:adapters], refs[adapters : adapters + parts]
    scale_ref, pick_ref, out_ref, rows_ref = refs[adapters + parts :]
    tokens = scale_ref.shape[0]
    groups = tokens // GROUP
    used = adapters * GROUP

    @pl.when(pl.program_id(0) == 0)
    def _():
        rows_ref[:, used + 2 * GROUP :, :] = jnp.zeros_like(rows_ref[:, used + 2 * GROUP :, :])

    base = bases[0][...].astype(jnp.float32)
    for part in bases[1:]:
        base = base + part[...].astype(jnp.float32)
    base = base * scale_ref[...]
    high = base.astype(jnp.bfloat16)
    low = (base - high.astype(jnp.float32)).astype(jnp.bfloat16)
    for g in range(groups):
        here = slice(g * GROUP, (g + 1) * GROUP)
        for a in range(adapters):
            rows_ref[g, a * GROUP : (a + 1) * GROUP, :] = deltas[a][here, :]
        rows_ref[g, used : used + GROUP, :] = high[here, :]
        rows_ref[g, used + GROUP : used + 2 * GROUP, :] = low[here, :]
    for g in range(groups):
        mixed = jnp.dot(pick_ref[g], rows_ref[g], preferred_element_type=jnp.float32)
        out_ref[g] = mixed.astype(jnp.bfloat16)


def mix(deltas, bases, scale, pick, half):
    tokens, width = deltas[0].shape[0], deltas[0].shape[1] // 2
    groups, rows, depth = pick.shape
    block = next(n for n in (640, 256, 128) if width % n == 0)
    steps = width // block
    column = pl.BlockSpec((tokens, block), lambda i: (0, half * steps + i))
    single = pl.BlockSpec((tokens, block), lambda i: (0, i))
    out = pl.pallas_call(
        functools.partial(mix_kernel, adapters=len(deltas), parts=len(bases)),
        grid=(steps,),
        in_specs=[column if value.shape[1] > width else single for value in (*deltas, *bases)]
        + [
            pl.BlockSpec((tokens, 1), lambda i: (0, 0)),
            pl.BlockSpec((groups, rows, depth), lambda i: (0, 0, 0)),
        ],
        out_specs=pl.BlockSpec((groups, rows, block), lambda i: (0, 0, i)),
        scratch_shapes=[pltpu.VMEM((groups, depth, block), jnp.bfloat16)],
        out_shape=jax.ShapeDtypeStruct((groups, rows, width), jnp.bfloat16),
        compiler_params=pltpu.CompilerParams(vmem_limit_bytes=40 * 1024 * 1024),
        cost_estimate=pl.CostEstimate(
            flops=2 * groups * rows * depth * width,
            bytes_accessed=2 * groups * rows * width,
            transcendentals=0,
        ),
    )(*deltas, *bases, scale, pick)
    return out.reshape(tokens, SLOTS, width)


def pick_matrix(
    token_index,
    prompt_token_length,
    prompt_of_request,
    adapter_of_request,
    adapter_slot_index,
    adapters,
    depth,
    order,
):
    tokens = token_index.shape[0]
    ends = jnp.cumsum(prompt_token_length)
    prompt_of = jnp.sum((token_index[:, None] >= ends[None, :]).astype(jnp.int32), axis=1)
    first = jnp.sum((prompt_of_request[None, :] < prompt_of[:, None]).astype(jnp.int32), axis=1)
    after = jnp.sum((prompt_of_request[None, :] <= prompt_of[:, None]).astype(jnp.int32), axis=1)
    hot = adapter_of_request[:, None] == jnp.arange(adapter_slot_index.shape[0], dtype=jnp.int32)[None, :]
    slot_of = jnp.sum(jnp.where(hot, adapter_slot_index[None, :], 0), axis=1)
    request = first[:, None] + jnp.arange(SLOTS, dtype=jnp.int32)[None, :]
    live = request < after[:, None]
    requests = jnp.arange(prompt_of_request.shape[0], dtype=jnp.int32)
    slot = jnp.sum(
        jnp.where(request[:, :, None] == requests[None, None, :], slot_of[None, None, :], 0), axis=2
    )
    place = (jnp.arange(tokens, dtype=jnp.int32) % GROUP)[:, None]
    column = jnp.where(live, order(slot) * GROUP + place, -1)
    columns = jnp.arange(depth, dtype=jnp.int32)[None, None, :]
    used = adapters * GROUP
    of_base = (columns >= used) & (columns < used + 2 * GROUP) & (columns % GROUP == place[:, :, None])
    pick = (columns == column[:, :, None]) | (of_base & live[:, :, None])
    return pick.astype(jnp.bfloat16).reshape(tokens // GROUP, GROUP * SLOTS, depth)


def body(
    prompt_token_states,
    gain,
    projection_weight,
    adapter_down_maps,
    adapter_up_maps,
    prompt_token_length,
    prompt_of_request,
    adapter_of_request,
    adapter_slot_index,
):
    rows, cols = lax.axis_size("row"), lax.axis_size("col")
    row, col = lax.axis_index("row"), lax.axis_index("col")
    lines = cols // 2
    line, side = col // 2, col % 2
    tokens, width = prompt_token_states.shape
    depth_in = projection_weight.shape[0]
    low_rank = adapter_down_maps.shape[2] // 2
    adapters = cols

    def send(value, pairs):
        flat = [(a * cols + b, c * cols + d) for (a, b), (c, d) in pairs]
        return lax.ppermute(value, ("row", "col"), flat)

    every = [(r, c) for r in range(rows) for c in range(cols)]

    def to_side(value):
        return send(value, [((r, c), (r, c ^ 1)) for r, c in every])

    def to_line(value, k):
        return send(value, [((r, c), (r, c ^ (2 * k))) for r, c in every])

    def to_owner(value, k):
        return send(
            value, [((r, 2 * (r ^ k) + s), (r, 2 * r + s)) for r in range(rows) for s in range(2)]
        )

    def to_far_rows(value):
        bit = 2
        while bit < rows:
            got = send(
                value,
                [
                    ((c // 2 ^ e, c), (c // 2 ^ e ^ bit, c))
                    for c in range(cols)
                    for e in range(0, bit, 2)
                ],
            )
            value = jnp.where((row ^ line) & bit != 0, got, value)
            bit *= 2
        return value

    def to_next_row(value):
        got = send(
            value,
            [((c // 2 ^ e, c), (c // 2 ^ e ^ 1, c)) for c in range(cols) for e in range(0, rows, 2)],
        )
        return jnp.where((row ^ line) & 1 != 0, got, value)

    def over_rows(value):
        return to_next_row(to_far_rows(value))

    def after(value, *others):
        return lax.optimization_barrier((value, *others))[0]

    def pairs_of(lines_pairs):
        return [
            ((r, 2 * a + s), (r, 2 * b + s)) for r in range(rows) for a, b in lines_pairs for s in range(2)
        ]

    across = pairs_of([(1, 2), (2, 1)])
    outward = pairs_of([(1, 0), (2, 3)])
    inner = (line == 1) | (line == 2)
    up_own = adapter_up_maps[0]
    weight = projection_weight.reshape(depth_in, 2 * width)

    states = prompt_token_states.astype(jnp.float32)
    gained = (states * gain.astype(jnp.float32)[None, :]).astype(jnp.bfloat16)

    def halves(values):
        mine = lax.dynamic_slice_in_dim(values, side * depth_in, depth_in, 2)
        theirs = lax.dynamic_slice_in_dim(values, (1 - side) * depth_in, depth_in, 2)
        return mine, send(theirs, [((c // 2, c), (c // 2, c ^ 1)) for c in range(cols)])

    def product(value):
        return jnp.dot(value, weight, preferred_element_type=jnp.float32)

    rest = [to_line(gained, k) for k in range(1, lines)]
    both = over_rows(jnp.stack(halves(gained[None])))
    other_down = to_side(after(adapter_down_maps[0], gained))
    up_other = to_side(after(up_own, gained))
    own_out = to_side(product(both[1, 0]).astype(jnp.bfloat16))
    own_kept = product(both[0, 0])

    late = lax.optimization_barrier((up_own, up_other, *rest))
    up_late, up_other, rest = late[0], late[1], late[2:]
    if lines == 4:
        near = to_line(jnp.stack([up_late, up_other]), 1)
        near, near_other = near[0], near[1]
        far_near = send(up_late, across)
    else:
        near = to_line(up_late, 1)

    mine, got = halves(jnp.stack(rest))
    mine_far = to_far_rows(mine)
    gathered = jnp.concatenate([gained, *rest], axis=0)
    gathered, other_down, up_other = lax.optimization_barrier((gathered, other_down, up_other))
    down = jnp.concatenate([adapter_down_maps[0], other_down], axis=1)
    partial = jnp.dot(gathered, down, preferred_element_type=jnp.float32)
    got, partial = lax.optimization_barrier((got, partial))
    partial = partial.reshape(lines, tokens, 4 * low_rank)
    parts = {
        m: lax.dynamic_index_in_dim(partial, row ^ line ^ m, 0, keepdims=False) for m in range(rows)
    }
    squares = after(jnp.sum(states * states, axis=1), partial)
    squares = jnp.pad(squares[None], ((0, 7), (0, 4 * low_rank - tokens)))
    bit = 1
    while bit < rows:
        leaving = [m for m in parts if m & bit]
        message = jnp.concatenate([parts.pop(m) for m in leaving] + [squares])
        arrived = send(message, [((r, c), (r ^ bit, c)) for r, c in every])
        for i, m in enumerate(leaving):
            parts[m ^ bit] = parts[m ^ bit] + arrived[i * tokens : (i + 1) * tokens]
        squares = squares + arrived[len(leaving) * tokens :]
        bit *= 2
    held = parts[0].astype(jnp.bfloat16)

    both = to_next_row(after(jnp.stack([mine_far, to_far_rows(got)]), held))
    outs = [product(both[1, k]).astype(jnp.bfloat16) for k in range(lines - 1)]
    kept = [product(both[0, k]) for k in range(lines - 1)]
    came = [None] * (lines - 1)
    for k in reversed(range(lines - 1)):
        came[k] = to_side(outs[k])

    ranks = [held] + [to_owner(held, k) for k in range(1, lines)]
    if lines == 4:
        far_far = send(near, across)
        first = send(far_near, outward)
        far_far, first, *ranks = lax.optimization_barrier((far_far, first, *ranks, came[-1]))[:-1]
        last = jnp.where(inner, far_far, send(far_far, outward))
        first = jnp.where(inner, far_near, first)
        blocks = [first, last]
        ups = [up_own, up_other, near, near_other]
    else:
        blocks = [near] + [to_line(up_own, k) for k in range(2, lines)]
        ups = [up_own, up_other]
    ranks = over_rows(jnp.stack(ranks))
    ranks = ranks.reshape(lines, tokens, 2, 2, low_rank).transpose(0, 2, 3, 1, 4)
    ranks = ranks.reshape(adapters, 2, tokens, low_rank)
    if lines == 4:
        far = jnp.where(inner, jnp.concatenate([ranks[6:], ranks[4:6]]), ranks[4:])
        ranks = jnp.concatenate([ranks[:4], far])

    for value in blocks[:-1]:
        ups += [value, to_side(after(value, came[-1]))]
    value = after(blocks[-1], came[-1])
    ups += [blocks[-1], [to_side(value[:1]), to_side(value[1:])]]

    if lines == 4:
        came = [after(value, far_far) for value in came]
    bases = [own_kept + own_out.astype(jnp.float32)]
    for k in reversed(range(lines - 1)):
        total = kept[k] + came[k].astype(jnp.float32)
        bases.append(to_line(total.astype(jnp.bfloat16), k + 1))

    def order(slot):
        place = slot ^ col
        return jnp.where(inner & (place >= 4), place ^ 2, place) if lines == 4 else place

    scale = lax.rsqrt(squares[0, :tokens] / (width * rows) + 1e-05)[:, None]
    depth = -(-(adapters * GROUP + 2 * GROUP) // 128) * 128
    token_index = col * tokens + jnp.arange(tokens, dtype=jnp.int32)
    pick = pick_matrix(
        token_index,
        prompt_token_length,
        prompt_of_request,
        adapter_of_request,
        adapter_slot_index,
        adapters,
        depth,
        order,
    )
    outs = []
    deltas = [corrections(ranks[e], ups[e], scale) for e in range(adapters) if not isinstance(ups[e], list)]
    for half in range(2):
        own = [
            corrections(ranks[e, half : half + 1], ups[e][half], scale)
            for e in range(adapters)
            if isinstance(ups[e], list)
        ]
        outs.append(mix(deltas + own, bases, scale, pick, half))
    return tuple(outs)


def solution(mesh):
    placed = (
        P("col", "row"),
        P("row"),
        P("col", None, "row"),
        P("col", "row", None),
        P("col", None, None, "row"),
        P(),
        P(),
        P(),
        P(),
    )
    return jax.shard_map(
        body,
        mesh=mesh,
        in_specs=placed,
        out_specs=(P("col", None, "row"), P("col", None, "row")),
        check_vma=False,
    )
```

```python
import functools

import jax
import jax.numpy as jnp
from jax import lax
from jax.experimental import pallas as pl
from jax.experimental.pallas import tpu as pltpu
from jax.sharding import PartitionSpec as P

SLOTS = 16
GROUP = 16


def delta_kernel(rank_ref, up_ref, scale_ref, out_ref):
    product = jnp.dot(rank_ref[0], up_ref[0], preferred_element_type=jnp.float32)
    out_ref[...] = (product * scale_ref[...]).astype(jnp.bfloat16)


def corrections(rank, up, scale):
    _, tokens, low_rank = rank.shape
    n, _, width = up.shape
    return pl.pallas_call(
        delta_kernel,
        grid=(n,),
        in_specs=[
            pl.BlockSpec((1, tokens, low_rank), lambda j: (j, 0, 0)),
            pl.BlockSpec((1, low_rank, width), lambda j: (j, 0, 0)),
            pl.BlockSpec((tokens, 1), lambda j: (0, 0)),
        ],
        out_specs=pl.BlockSpec((tokens, width), lambda j: (0, j)),
        out_shape=jax.ShapeDtypeStruct((tokens, n * width), jnp.bfloat16),
        compiler_params=pltpu.CompilerParams(vmem_limit_bytes=24 * 1024 * 1024),
        cost_estimate=pl.CostEstimate(
            flops=2 * n * tokens * low_rank * width,
            bytes_accessed=2 * n * (tokens * width + low_rank * width),
            transcendentals=0,
        ),
    )(rank, up, scale)


def mix_kernel(*refs, adapters, parts, steps):
    deltas, bases = refs[:adapters], refs[adapters : adapters + parts]
    last_ref, scale_ref, pick_ref, query_ref, value_ref, rows_ref = refs[adapters + parts :]
    half = pl.program_id(0) // steps
    tokens = scale_ref.shape[0]
    groups = tokens // GROUP
    used = adapters * GROUP

    @pl.when(pl.program_id(0) == 0)
    def _():
        rows_ref[:, used + 2 * GROUP :, :] = jnp.zeros_like(rows_ref[:, used + 2 * GROUP :, :])

    base = bases[0][...].astype(jnp.float32)
    for part in bases[1:]:
        base = base + part[...].astype(jnp.float32)
    base = base * scale_ref[...]
    high = base.astype(jnp.bfloat16)
    low = (base - high.astype(jnp.float32)).astype(jnp.bfloat16)
    for g in range(groups):
        here = slice(g * GROUP, (g + 1) * GROUP)
        for a in range(adapters):
            delta = deltas[a][here, :]
            if a == adapters - 1:
                delta = jnp.where(half == 0, delta, last_ref[here, :])
            rows_ref[g, a * GROUP : (a + 1) * GROUP, :] = delta
        rows_ref[g, used : used + GROUP, :] = high[here, :]
        rows_ref[g, used + GROUP : used + 2 * GROUP, :] = low[here, :]

    def fill(out_ref):
        for g in range(groups):
            mixed = jnp.dot(pick_ref[g], rows_ref[g], preferred_element_type=jnp.float32)
            out_ref[g] = mixed.astype(jnp.bfloat16)

    pl.when(half == 0)(lambda: fill(query_ref))
    pl.when(half == 1)(lambda: fill(value_ref))


def mix(deltas, bases, scale, pick):
    tokens, width = deltas[-1].shape
    groups, rows, depth = pick.shape
    block = next(n for n in (640, 256, 128) if width % n == 0)
    steps = width // block
    column = pl.BlockSpec((tokens, block), lambda i: (0, i))
    query = pl.BlockSpec((tokens, block), lambda i: (0, jnp.minimum(i, steps - 1)))
    value = pl.BlockSpec((tokens, block), lambda i: (0, jnp.maximum(i - steps, 0)))
    shape = jax.ShapeDtypeStruct((groups, rows, width), jnp.bfloat16)
    outs = pl.pallas_call(
        functools.partial(mix_kernel, adapters=len(deltas) - 1, parts=len(bases), steps=steps),
        grid=(2 * steps,),
        in_specs=[column] * (len(deltas) - 2)
        + [query]
        + [column] * len(bases)
        + [
            value,
            pl.BlockSpec((tokens, 1), lambda i: (0, 0)),
            pl.BlockSpec((groups, rows, depth), lambda i: (0, 0, 0)),
        ],
        out_specs=[
            pl.BlockSpec((groups, rows, block), lambda i: (0, 0, jnp.minimum(i, steps - 1))),
            pl.BlockSpec((groups, rows, block), lambda i: (0, 0, jnp.maximum(i - steps, 0))),
        ],
        scratch_shapes=[pltpu.VMEM((groups, depth, block), jnp.bfloat16)],
        out_shape=[shape, shape],
        compiler_params=pltpu.CompilerParams(vmem_limit_bytes=58 * 1024 * 1024),
        cost_estimate=pl.CostEstimate(
            flops=4 * groups * rows * depth * width,
            bytes_accessed=4 * groups * rows * width,
            transcendentals=0,
        ),
    )(*deltas[:-1], *bases, deltas[-1], scale, pick)
    return tuple(out.reshape(tokens, SLOTS, width) for out in outs)


def pick_matrix(
    token_index,
    prompt_token_length,
    prompt_of_request,
    adapter_of_request,
    adapter_slot_index,
    adapters,
    depth,
    order,
):
    tokens = token_index.shape[0]
    ends = jnp.cumsum(prompt_token_length)
    prompt_of = jnp.sum((token_index[:, None] >= ends[None, :]).astype(jnp.int32), axis=1)
    first = jnp.sum((prompt_of_request[None, :] < prompt_of[:, None]).astype(jnp.int32), axis=1)
    after = jnp.sum((prompt_of_request[None, :] <= prompt_of[:, None]).astype(jnp.int32), axis=1)
    hot = adapter_of_request[:, None] == jnp.arange(adapter_slot_index.shape[0], dtype=jnp.int32)[None, :]
    slot_of = jnp.sum(jnp.where(hot, adapter_slot_index[None, :], 0), axis=1)
    request = first[:, None] + jnp.arange(SLOTS, dtype=jnp.int32)[None, :]
    live = request < after[:, None]
    requests = jnp.arange(prompt_of_request.shape[0], dtype=jnp.int32)
    slot = jnp.sum(
        jnp.where(request[:, :, None] == requests[None, None, :], slot_of[None, None, :], 0), axis=2
    )
    place = (jnp.arange(tokens, dtype=jnp.int32) % GROUP)[:, None]
    column = jnp.where(live, order(slot) * GROUP + place, -1)
    columns = jnp.arange(depth, dtype=jnp.int32)[None, None, :]
    used = adapters * GROUP
    of_base = (columns >= used) & (columns < used + 2 * GROUP) & (columns % GROUP == place[:, :, None])
    pick = (columns == column[:, :, None]) | (of_base & live[:, :, None])
    return pick.astype(jnp.bfloat16).reshape(tokens // GROUP, GROUP * SLOTS, depth)


def body(
    prompt_token_states,
    gain,
    projection_weight,
    adapter_down_maps,
    adapter_up_maps,
    prompt_token_length,
    prompt_of_request,
    adapter_of_request,
    adapter_slot_index,
):
    rows, cols = lax.axis_size("row"), lax.axis_size("col")
    row, col = lax.axis_index("row"), lax.axis_index("col")
    lines = cols // 2
    line, side = col // 2, col % 2
    tokens, width = prompt_token_states.shape
    depth_in = projection_weight.shape[0]
    low_rank = adapter_down_maps.shape[2] // 2
    adapters = cols

    def send(value, pairs):
        flat = [(a * cols + b, c * cols + d) for (a, b), (c, d) in pairs]
        return lax.ppermute(value, ("row", "col"), flat)

    every = [(r, c) for r in range(rows) for c in range(cols)]

    def to_side(value):
        return send(value, [((r, c), (r, c ^ 1)) for r, c in every])

    def to_line(value, k):
        return send(value, [((r, c), (r, c ^ (2 * k))) for r, c in every])

    def to_owner(value, k):
        return send(
            value, [((r, 2 * (r ^ k) + s), (r, 2 * r + s)) for r in range(rows) for s in range(2)]
        )

    def to_far_rows(value):
        bit = 2
        while bit < rows:
            got = send(
                value,
                [
                    ((c // 2 ^ e, c), (c // 2 ^ e ^ bit, c))
                    for c in range(cols)
                    for e in range(0, bit, 2)
                ],
            )
            value = jnp.where((row ^ line) & bit != 0, got, value)
            bit *= 2
        return value

    def to_next_row(value):
        got = send(
            value,
            [((c // 2 ^ e, c), (c // 2 ^ e ^ 1, c)) for c in range(cols) for e in range(0, rows, 2)],
        )
        return jnp.where((row ^ line) & 1 != 0, got, value)

    def over_rows(value):
        return to_next_row(to_far_rows(value))

    def after(value, *others):
        return lax.optimization_barrier((value, *others))[0]

    def pairs_of(lines_pairs):
        return [
            ((r, 2 * a + s), (r, 2 * b + s)) for r in range(rows) for a, b in lines_pairs for s in range(2)
        ]

    across = pairs_of([(1, 2), (2, 1)])
    outward = pairs_of([(1, 0), (2, 3)])
    inner = (line == 1) | (line == 2)
    up_own = adapter_up_maps[0]
    weight = projection_weight.reshape(depth_in, 2 * width)

    states = prompt_token_states.astype(jnp.float32)
    gained = (states * gain.astype(jnp.float32)[None, :]).astype(jnp.bfloat16)

    def halves(values):
        mine = lax.dynamic_slice_in_dim(values, side * depth_in, depth_in, 2)
        theirs = lax.dynamic_slice_in_dim(values, (1 - side) * depth_in, depth_in, 2)
        return mine, send(theirs, [((c // 2, c), (c // 2, c ^ 1)) for c in range(cols)])

    def product(value):
        return jnp.dot(value, weight, preferred_element_type=jnp.float32)

    rest = [to_line(gained, k) for k in range(1, lines)]
    both = over_rows(jnp.stack(halves(gained[None])))
    other_down = to_side(after(adapter_down_maps[0], gained))
    up_other = to_side(after(up_own, gained))
    own_out = to_side(product(both[1, 0]).astype(jnp.bfloat16))
    own_kept = product(both[0, 0])

    late = lax.optimization_barrier((up_own, up_other, *rest))
    up_late, up_other, rest = late[0], late[1], late[2:]
    if lines == 4:
        near = to_line(jnp.stack([up_late, up_other]), 1)
        near, near_other = near[0], near[1]
        far_near = send(up_late, across)
    else:
        near = to_line(up_late, 1)

    mine, got = halves(jnp.stack(rest))
    mine_far = to_far_rows(mine)
    gathered = jnp.concatenate([gained, *rest], axis=0)
    gathered, other_down, up_other = lax.optimization_barrier((gathered, other_down, up_other))
    down = jnp.concatenate([adapter_down_maps[0], other_down], axis=1)
    partial = jnp.dot(gathered, down, preferred_element_type=jnp.float32)
    got, partial = lax.optimization_barrier((got, partial))
    partial = partial.reshape(lines, tokens, 4 * low_rank)
    parts = {
        m: lax.dynamic_index_in_dim(partial, row ^ line ^ m, 0, keepdims=False) for m in range(rows)
    }
    squares = after(jnp.sum(states * states, axis=1), partial)
    squares = jnp.pad(squares[None], ((0, 7), (0, 4 * low_rank - tokens)))
    bit = 1
    while bit < rows:
        leaving = [m for m in parts if m & bit]
        message = jnp.concatenate([parts.pop(m) for m in leaving] + [squares])
        arrived = send(message, [((r, c), (r ^ bit, c)) for r, c in every])
        for i, m in enumerate(leaving):
            parts[m ^ bit] = parts[m ^ bit] + arrived[i * tokens : (i + 1) * tokens]
        squares = squares + arrived[len(leaving) * tokens :]
        bit *= 2
    held = parts[0].astype(jnp.bfloat16)

    both = to_next_row(after(jnp.stack([mine_far, to_far_rows(got)]), held))
    outs = [product(both[1, k]).astype(jnp.bfloat16) for k in range(lines - 1)]
    kept = [product(both[0, k]) for k in range(lines - 1)]
    came = [None] * (lines - 1)
    for k in reversed(range(lines - 1)):
        came[k] = to_side(outs[k])

    ranks = [held] + [to_owner(held, k) for k in range(1, lines)]
    if lines == 4:
        far_far = send(near, across)
        first = send(far_near, outward)
        far_far, first, *ranks = lax.optimization_barrier((far_far, first, *ranks, came[-1]))[:-1]
        last = jnp.where(inner, far_far, send(far_far, outward))
        first = jnp.where(inner, far_near, first)
        blocks = [first, last]
        ups = [up_own, up_other, near, near_other]
    else:
        blocks = [near] + [to_line(up_own, k) for k in range(2, lines)]
        ups = [up_own, up_other]
    ranks = over_rows(jnp.stack(ranks))
    ranks = ranks.reshape(lines, tokens, 2, 2, low_rank).transpose(0, 2, 3, 1, 4)
    ranks = ranks.reshape(adapters, 2, tokens, low_rank)
    if lines == 4:
        far = jnp.where(inner, jnp.concatenate([ranks[6:], ranks[4:6]]), ranks[4:])
        ranks = jnp.concatenate([ranks[:4], far])

    for value in blocks[:-1]:
        ups += [value, to_side(after(value, came[-1]))]
    value = after(blocks[-1], came[-1])
    ups += [blocks[-1], [to_side(value[:1]), to_side(value[1:])]]

    if lines == 4:
        came = [after(value, far_far) for value in came]
    bases = [own_kept + own_out.astype(jnp.float32)]
    for k in reversed(range(lines - 1)):
        total = kept[k] + came[k].astype(jnp.float32)
        bases.append(to_line(total.astype(jnp.bfloat16), k + 1))

    def order(slot):
        place = slot ^ col
        return jnp.where(inner & (place >= 4), place ^ 2, place) if lines == 4 else place

    scale = lax.rsqrt(squares[0, :tokens] / (width * rows) + 1e-05)[:, None]
    depth = -(-(adapters * GROUP + 2 * GROUP) // 128) * 128
    token_index = col * tokens + jnp.arange(tokens, dtype=jnp.int32)
    pick = pick_matrix(
        token_index,
        prompt_token_length,
        prompt_of_request,
        adapter_of_request,
        adapter_slot_index,
        adapters,
        depth,
        order,
    )
    deltas = [corrections(ranks[e], ups[e], scale) for e in range(adapters - 1)]
    last = ups[-1] if isinstance(ups[-1], list) else [ups[-1][:1], ups[-1][1:]]
    deltas += [corrections(ranks[-1, half : half + 1], last[half], scale) for half in range(2)]
    return mix(deltas, bases, scale, pick)


def solution(mesh):
    placed = (
        P("col", "row"),
        P("row"),
        P("col", None, "row"),
        P("col", "row", None),
        P("col", None, None, "row"),
        P(),
        P(),
        P(),
        P(),
    )
    return jax.shard_map(
        body,
        mesh=mesh,
        in_specs=placed,
        out_specs=(P("col", None, "row"), P("col", None, "row")),
        check_vma=False,
    )
```
